256 devices in a mesh: dp: 16 (over x, z_lo, core), tensor: 16 (over z_hi, y).
Axes of the slice: x: 4, y: 4, z: 8 (z_hi: 4, z_lo: 2; z = z_hi * 2 + z_lo), core: 2. Of those that a mesh axis runs over, the one named last changes fastest.
Arguments:
- tokens: bfloat16 [32768, 3072], P(('dp', 'tensor')), may hold values from -6 to 6
- routes: int32 [32768, 2], P(('dp', 'tensor')), may hold values from 0 to 7, as said below
- router: bfloat16 [3072, 8], replicated, may hold values from -0.109375 to 0.109375
- w_up: bfloat16 [3072, 16384], P('dp', 'tensor'), may hold values from -0.109375 to 0.109375
- w_down: bfloat16 [16384, 3072], P(('tensor', 'dp')), may hold values from -0.046875 to 0.046875
- grad_parts: bfloat16 [16, 16384, 3072], P('dp', 'tensor'), may hold values from -6 to 6
- master: float32 [16384, 3072], P(('tensor', 'dp')), may hold values from -4 to 4
- moment_one: bfloat16 [16384, 3072], P(('tensor', 'dp')), may hold values from -3 to 3
- moment_two: float32 [16384, 3072], P(('tensor', 'dp')), may hold values from 0.01 to 1
Outputs:
- mixed: bfloat16 [32768, 3072], P(('dp', 'tensor'))
- new_master: float32 [16384, 3072], P(('tensor', 'dp'))
- new_moment_one: bfloat16 [16384, 3072], P(('tensor', 'dp'))
- new_moment_two: float32 [16384, 3072], P(('tensor', 'dp'))
The draws below stay inside these ranges and needn't reach their ends.
Inputs may be any that keep to these rules, and one draw needn't show every extreme that they name: `routes`: each row names two different experts. Among the 128 rows of one device at most 48 name expert 0, and on some device exactly 48.
All inputs are finite; a program needn't handle non-finite values.
Results may differ from the reference program's by a relative error of at most 0.02.
Values may be sent and summed in bfloat16 or wider, within the bound.
No kernel may reach another device: no remote copies, remote signals or barrier semaphores. Data moves between devices by JAX's collectives and lax.ppermute only.
A program may use at most 128 MiB of HBM per device.

```python
import math
import jax
import jax.numpy as jnp
from jax import lax

D = 3072
FF = 16384
EXPERTS = 8
TOK_DEV = 128
CAP = 48
TOKENS = 32768
N_DP = 16
N_TENSOR = 16


def draw_routes(key, part):
    key = jax.random.fold_in(key, 7)
    key_count, key_order, key_partner, key_other, key_swap = jax.random.split(key, 5)
    blocks = TOKENS // TOK_DEV
    counts = jax.random.randint(key_count, (blocks,), CAP // 2, CAP + 1)
    counts = counts.at[0].set(CAP)

    def shuffled(one_key):
        return jax.random.permutation(one_key, TOK_DEV)
    rank_table = jax.vmap(shuffled)(jax.random.split(key_order, blocks))
    routed = (rank_table < counts[:, None]).reshape(TOKENS)
    partner = jax.random.randint(key_partner, (TOKENS,), 1, EXPERTS)
    offset_draw = jax.random.randint(key_other, (TOKENS,), 1, EXPERTS - 1)
    second = 1 + (partner - 1 + offset_draw) % (EXPERTS - 1)
    leading = jnp.where(routed, 0, partner)
    trailing = jnp.where(routed, partner, second)
    swapped = jax.random.randint(key_swap, (TOKENS,), 0, 2) == 1
    first_col = jnp.where(swapped, trailing, leading)
    second_col = jnp.where(swapped, leading, trailing)
    return jnp.stack([first_col, second_col], axis=1).astype(jnp.int32)


def strengthened(result, own_key, source, target, parts, factor):
    def block_of(axis_at):
        return (jnp.arange(result.shape[axis_at]) // (result.shape[axis_at] // parts)).reshape((-1,) + (1,) * (result.ndim - 1 - axis_at))

    one_side = jax.random.permutation(own_key, parts)[block_of(target)]
    second = (block_of(target) + parts // 2) % parts
    return jnp.where((block_of(source) == one_side) | (block_of(source) == second), factor * result, result)


def level_of(own_key, shape, cuts, smallest, top_value):
    loudness = 1.0
    for position, blocks in cuts:
        heights = jax.random.uniform(jax.random.fold_in(jax.random.fold_in(own_key, 6), position), (blocks,), jnp.float32, smallest / len(cuts), top_value / len(cuts))
        loudness = loudness * jnp.repeat(jnp.exp(heights), shape[position] // blocks).reshape((-1,) + (1,) * (len(shape) - 1 - position))
    return loudness


def gaussian(own_key, shape, scale, most, shards=(), held_as=jnp.bfloat16):
    factor_of = level_of(own_key, shape, shards, -0.22, 0.18) if shards else 1.0
    values = jax.random.normal(own_key, shape, jnp.float32) * scale * factor_of
    return jnp.minimum(jnp.maximum(values, -most), most).astype(held_as)


def noise_with(own_key, shape, deviation, most, cuts, heavy, held_as=jnp.bfloat16):
    values = deviation * jax.random.normal(own_key, shape, jnp.float32)
    if cuts:
        values = values * level_of(own_key, shape, cuts, -0.22, 0.18)
    return jnp.clip(strengthened(values, jax.random.fold_in(own_key, 3), *heavy), -most, most).astype(held_as)


def setup_inputs(seed: int = 0) -> dict:
    seeds = jax.random.split(jax.random.key(seed), 10)
    return {
        "tokens": gaussian(seeds[0], (TOKENS, D), 1.0, 6.0, ((0, 256),)),
        "routes": draw_routes(jax.random.fold_in(seeds[9], 71), 0),
        "router": gaussian(seeds[2], (D, EXPERTS), D ** -0.5, 0.109375),
        "w_up": gaussian(seeds[3], (D, FF), D ** -0.5, 0.109375, ((0, 16), (1, 16))),
        "w_down": gaussian(seeds[4], (FF, D), FF ** -0.5, 0.046875, ((0, 256),)),
        "grad_parts": noise_with(seeds[5], (N_DP, FF, D), 1.0, 6.0, ((0, 16), (1, 16)), (0, 1, 16, 2.0)),
        "master": gaussian(seeds[6], (FF, D), 0.5, 4.0, ((0, 256),), jnp.float32),
        "moment_one": gaussian(seeds[7], (FF, D), 0.3, 3.0, ((0, 256),)),
        "moment_two": jnp.clip(jnp.exp(math.log(1.0) - 4.6051702 * jax.random.uniform(seeds[8], (FF, D), jnp.float32) ** level_of(seeds[8], (FF, D), ((0, 256),), -0.2, 0.2)), 0.01, 1.0),
    }


beta_first = 0.9
beta_second = 0.999
learn_rate = 0.01
decay_rate = 0.1
adam_eps = 1e-08
bias_first = 1.0 - (0.9 ** 10) ** 10
bias_second = 1.0 - (0.999 ** 10) ** 10

def gating_of(tokens, routes, router):
    logits = jnp.dot(tokens, router, preferred_element_type=jnp.float32)
    expert_iota = jnp.arange(logits.shape[1], dtype=jnp.int32)
    chosen = lax.optimization_barrier(jnp.sum(jnp.where(routes[:, :, None] == expert_iota, logits[:, None, :], 0.0), axis=2))
    is_first = routes[:, 0] == 0
    routed = is_first | (routes[:, 1] == 0)
    own_logit = jnp.where(is_first, chosen[:, 0], chosen[:, 1])
    partner = jnp.where(is_first, chosen[:, 1], chosen[:, 0])
    gating = jnp.where(routed, jax.nn.sigmoid(own_logit - partner), 0.0)
    return (routed, gating)

def adam_step(grad_total, master, moment_one, moment_two):
    new_one = (beta_first * moment_one.astype(jnp.float32) + (1.0 - beta_first) * grad_total).astype(jnp.bfloat16)
    new_two = beta_second * moment_two + (1.0 - beta_second) * grad_total * grad_total
    update = new_one.astype(jnp.float32) / bias_first / (jnp.sqrt(new_two / bias_second) + adam_eps)
    new_master = master - learn_rate * (update + decay_rate * master)
    return (new_master, new_one, new_two)

def reference(tokens, routes, router, w_up, w_down, grad_parts, master, moment_one, moment_two):
    routed, gating = gating_of(tokens, routes, router)
    blocks = N_DP * N_TENSOR
    routed_blocks = routed.reshape(blocks, TOK_DEV)
    slot_index = (jnp.cumsum(routed_blocks.astype(jnp.int32), axis=1) - 1).astype(jnp.int32)
    width = FF // N_TENSOR

    def place(block_tokens, block_target):
        return jnp.zeros((CAP, D), block_tokens.dtype).at[block_target].set(block_tokens, mode='drop')

    def fetch(out_rows, slots):
        return jnp.take(out_rows, jnp.clip(slots, 0, CAP - 1), axis=0)

    def group_forward(inputs):
        group_tokens, group_slots, group_routed, group_gating = inputs
        target = jnp.where(group_routed, group_slots, CAP).astype(jnp.int32)
        dispatched = jax.vmap(place)(group_tokens, target).reshape(N_TENSOR * CAP, D)
        up_out = jnp.dot(dispatched, w_up, preferred_element_type=jnp.float32)
        hidden = jax.nn.gelu(up_out, approximate=False).astype(jnp.bfloat16)

        def add_group(running, group_number):
            offset = (group_number * width).astype(jnp.int32)
            hid_cols = lax.dynamic_slice_in_dim(hidden, offset, width, 1)
            rows_part = lax.dynamic_slice_in_dim(w_down, offset, width, 0)
            term = jnp.dot(hid_cols, rows_part, preferred_element_type=jnp.float32).astype(jnp.bfloat16)
            term = lax.optimization_barrier(term)
            return (running + term.astype(jnp.float32), None)
        summed, _ = lax.scan(add_group, jnp.zeros((N_TENSOR * CAP, D), jnp.float32), jnp.arange(N_TENSOR, dtype=jnp.int32))
        summed = summed.reshape(N_TENSOR, CAP, D)
        picked = jax.vmap(fetch)(summed, group_slots)
        return (picked * group_gating[:, :, None]).astype(jnp.bfloat16)
    mixed = lax.map(group_forward, (tokens.reshape(N_DP, N_TENSOR, TOK_DEV, D), slot_index.reshape(N_DP, N_TENSOR, TOK_DEV), routed_blocks.reshape(N_DP, N_TENSOR, TOK_DEV), gating.reshape(N_DP, N_TENSOR, TOK_DEV)))
    mixed = mixed.reshape(TOKENS, D)
    grad_total = lax.optimization_barrier(jnp.sum(grad_parts.astype(jnp.float32), axis=0))
    new_master, new_one, new_two = adam_step(grad_total, master, moment_one, moment_two)
    return (mixed, new_master, new_one, new_two)
```

```python
import jax
import jax.numpy as jnp
from jax import lax
from jax.sharding import PartitionSpec as P

CAP = 48
D = 3072
N_X, N_ZL, N_C = 4, 2, 2
N_ZH, N_Y = 4, 4
DOWN_CHUNKS = 2

beta_first = 0.9
beta_second = 0.999
learn_rate = 0.01
decay_rate = 0.1
adam_eps = 1e-08
bias_first = 1.0 - (0.9**10) ** 10
bias_second = 1.0 - (0.999**10) ** 10


def dp_of(x, zl, c):
    return (x % N_X) * 4 + (zl % N_ZL) * 2 + c % N_C


def tensor_of(zh, y):
    return (zh % N_ZH) * 4 + y % N_Y


def get_dp(value, x=0, zl=0, c=0):
    pairs = [
        (dp_of(i + x, j + zl, k + c), dp_of(i, j, k))
        for i in range(N_X)
        for j in range(N_ZL)
        for k in range(N_C)
    ]
    return lax.ppermute(value, "dp", pairs)


def get_tensor(value, zh=0, y=0):
    pairs = [(tensor_of(i + zh, j + y), tensor_of(i, j)) for i in range(N_ZH) for j in range(N_Y)]
    return lax.ppermute(value, "tensor", pairs)


def gating_of(tokens, routes, router):
    logits = jnp.dot(tokens, router, preferred_element_type=jnp.float32)
    expert_iota = jnp.arange(logits.shape[1], dtype=jnp.int32)
    chosen = jnp.sum(jnp.where(routes[:, :, None] == expert_iota, logits[:, None, :], 0.0), axis=2)
    is_first = routes[:, 0] == 0
    routed = is_first | (routes[:, 1] == 0)
    own_logit = jnp.where(is_first, chosen[:, 0], chosen[:, 1])
    partner = jnp.where(is_first, chosen[:, 1], chosen[:, 0])
    gating = jnp.where(routed, jax.nn.sigmoid(own_logit - partner), 0.0)
    return (routed, gating)


def adam_step(grad_total, master, moment_one, moment_two):
    new_one = (
        beta_first * moment_one.astype(jnp.float32) + (1.0 - beta_first) * grad_total
    ).astype(jnp.bfloat16)
    new_two = beta_second * moment_two + (1.0 - beta_second) * grad_total * grad_total
    update = new_one.astype(jnp.float32) / bias_first / (jnp.sqrt(new_two / bias_second) + adam_eps)
    new_master = master - learn_rate * (update + decay_rate * master)
    return (new_master, new_one, new_two)


def relative_columns(rows, x, zl, c):
    rolled = lax.dynamic_slice_in_dim(jnp.concatenate([rows, rows], axis=1), x * 768, D, axis=1)
    r = rolled.reshape(rows.shape[0], N_X, N_ZL, N_C, 192)
    r = jnp.where(zl == 0, r, r[:, :, ::-1])
    r = jnp.where(c == 0, r, r[:, :, :, ::-1])
    return r.transpose(0, 3, 1, 2, 4).reshape(rows.shape[0], D)


def hidden_order(x, zl, c):
    p = jnp.arange(1024, dtype=jnp.int32)
    block, inside = p // 64, p % 64
    rc, rx, rz = block // 8, (block // 2) % 4, block % 2
    source = (((x + rx) % 4) * 4 + ((zl + rz) % 2) * 2 + (c + rc) % 2) * 64 + inside
    return (jnp.arange(1024, dtype=jnp.int32)[:, None] == source[None, :]).astype(jnp.bfloat16)


def total(parts):
    acc = parts[0].astype(jnp.float32)
    for part in parts[1:]:
        acc = acc + part.astype(jnp.float32)
    return acc


def local(tokens, routes, router, w_up, w_down, grad_parts, master, moment_one, moment_two):
    here = lax.axis_index("dp")
    x, zl, c = here // 4, (here // 2) % 2, here % 2

    routed, gating = gating_of(tokens, routes, router)
    slot_index = jnp.cumsum(routed.astype(jnp.int32)) - 1
    slot_iota = jnp.arange(CAP, dtype=jnp.int32)
    picks = ((slot_index[None, :] == slot_iota[:, None]) & routed[None, :]).astype(jnp.bfloat16)
    picked_rows = jnp.dot(picks, tokens, preferred_element_type=jnp.float32).astype(jnp.bfloat16)
    picked_rows = relative_columns(picked_rows, x, zl, c)

    halves = []
    for h in range(2):
        own = picked_rows[:, h * 1536 : (h + 1) * 1536]
        zrows = jnp.concatenate([own] + [get_tensor(own, zh=k) for k in (1, 3, 2)], axis=0)
        yrows = [zrows] + [get_tensor(zrows, y=k) for k in (1, 3, 2)]
        halves.append(jnp.concatenate(yrows, axis=0))

    up_z = jnp.concatenate([w_up, get_dp(w_up, zl=1)], axis=0)
    up_own = jnp.concatenate([up_z] + [get_dp(up_z, x=k) for k in (1, 2, 3)], axis=0)
    up_other = get_dp(up_own, c=1)

    down_z = jnp.concatenate([w_down, get_dp(w_down, zl=1)], axis=0)
    width = D // DOWN_CHUNKS
    downs = []
    for q in range(DOWN_CHUNKS):
        piece = down_z[:, q * width : (q + 1) * width]
        own = jnp.concatenate([piece] + [get_dp(piece, x=k) for k in (1, 2, 3)], axis=0)
        downs.append((own, get_dp(own, c=1)))

    grads = grad_parts[0].reshape(8, 2, 64, D)
    keep = lax.dynamic_index_in_dim(grads, c, axis=1, keepdims=False)
    give = lax.dynamic_index_in_dim(grads, 1 - c, axis=1, keepdims=False)
    core_sum = total([keep, get_dp(give, c=1)]).astype(jnp.bfloat16).reshape(512, D)

    up_out = jnp.dot(halves[0], up_own, preferred_element_type=jnp.float32)
    up_out = up_out + jnp.dot(halves[1], up_other, preferred_element_type=jnp.float32)
    hidden = jax.nn.gelu(up_out, approximate=False).astype(jnp.bfloat16)
    order = hidden_order(x, zl, c)
    hidden = jnp.dot(hidden, order, preferred_element_type=jnp.float32).astype(jnp.bfloat16)
    hidden = lax.optimization_barrier(hidden)

    owned = []
    for q in range(DOWN_CHUNKS):
        own, other = downs[q]
        partial = jnp.dot(hidden[:, :512], own, preferred_element_type=jnp.float32)
        partial = partial + jnp.dot(hidden[:, 512:], other, preferred_element_type=jnp.float32)
        partial = lax.optimization_barrier(partial.astype(jnp.bfloat16)).reshape(4, 192, width)
        came = [partial[0]] + [get_tensor(partial[i], y=-k) for i, k in ((1, 1), (2, 3), (3, 2))]
        ysum = lax.optimization_barrier(total(came).astype(jnp.bfloat16)).reshape(4, CAP, width)
        came = [ysum[0]] + [get_tensor(ysum[i], zh=-k) for i, k in ((1, 1), (2, 3), (3, 2))]
        owned.append(total(came))
    owned = jnp.concatenate(owned, axis=1)
    combined = jnp.take(owned, jnp.clip(slot_index, 0, CAP - 1), axis=0)
    mixed = (combined * gating[:, None]).astype(jnp.bfloat16)

    core_sum, _ = lax.optimization_barrier((core_sum, downs[-1][0]))
    xgroups = [[dp_of(i, j, k) for i in range(N_X)] for j in range(N_ZL) for k in range(N_C)]
    x_sum = lax.psum_scatter(
        core_sum, "dp", scatter_dimension=0, tiled=True, axis_index_groups=xgroups
    ).reshape(2, 64, D)
    keep = lax.dynamic_index_in_dim(x_sum, zl, axis=0, keepdims=False)
    give = lax.dynamic_index_in_dim(x_sum, 1 - zl, axis=0, keepdims=False)
    grad_total = total([keep, get_dp(give, zl=1)])
    new_master, new_one, new_two = adam_step(grad_total, master, moment_one, moment_two)
    return (mixed, new_master, new_one, new_two)


def solution(mesh):
    placed = (
        P(("dp", "tensor"), None),
        P(("dp", "tensor"), None),
        P(),
        P("dp", "tensor"),
        P(("tensor", "dp"), None),
        P("dp", "tensor", None),
        P(("tensor", "dp"), None),
        P(("tensor", "dp"), None),
        P(("tensor", "dp"), None),
    )
    return jax.shard_map(
        local,
        mesh=mesh,
        in_specs=placed,
        out_specs=(
            P(("dp", "tensor"), None),
            P(("tensor", "dp"), None),
            P(("tensor", "dp"), None),
            P(("tensor", "dp"), None),
        ),
        check_vma=False,
    )
```

```python
import jax
import jax.numpy as jnp
from jax import lax
from jax.experimental import pallas as pl
from jax.experimental.pallas import tpu as pltpu
from jax.sharding import PartitionSpec as P

CAP = 48
D = 3072
N_X, N_ZL, N_C = 4, 2, 2
N_ZH, N_Y = 4, 4

beta_first = 0.9
beta_second = 0.999
learn_rate = 0.01
decay_rate = 0.1
adam_eps = 1e-08
bias_first = 1.0 - (0.9**10) ** 10
bias_second = 1.0 - (0.999**10) ** 10


def dp_of(x, zl, c):
    return (x % N_X) * 4 + (zl % N_ZL) * 2 + c % N_C


def tensor_of(zh, y):
    return (zh % N_ZH) * 4 + y % N_Y


def get_dp(value, x=0, zl=0, c=0):
    pairs = [
        (dp_of(i + x, j + zl, k + c), dp_of(i, j, k))
        for i in range(N_X)
        for j in range(N_ZL)
        for k in range(N_C)
    ]
    return lax.ppermute(value, "dp", pairs)


def get_tensor(value, zh=0, y=0):
    pairs = [(tensor_of(i + zh, j + y), tensor_of(i, j)) for i in range(N_ZH) for j in range(N_Y)]
    return lax.ppermute(value, "tensor", pairs)


def gating_of(tokens, routes, router):
    logits = jnp.dot(tokens, router, preferred_element_type=jnp.float32)
    expert_iota = jnp.arange(logits.shape[1], dtype=jnp.int32)
    chosen = jnp.sum(jnp.where(routes[:, :, None] == expert_iota, logits[:, None, :], 0.0), axis=2)
    is_first = routes[:, 0] == 0
    routed = is_first | (routes[:, 1] == 0)
    own_logit = jnp.where(is_first, chosen[:, 0], chosen[:, 1])
    partner = jnp.where(is_first, chosen[:, 1], chosen[:, 0])
    gating = jnp.where(routed, jax.nn.sigmoid(own_logit - partner), 0.0)
    return (routed, gating)


def adam_step(grad_total, master, moment_one, moment_two):
    new_one = (
        beta_first * moment_one.astype(jnp.float32) + (1.0 - beta_first) * grad_total
    ).astype(jnp.bfloat16)
    new_two = beta_second * moment_two + (1.0 - beta_second) * grad_total * grad_total
    update = new_one.astype(jnp.float32) / bias_first / (jnp.sqrt(new_two / bias_second) + adam_eps)
    new_master = master - learn_rate * (update + decay_rate * master)
    return (new_master, new_one, new_two)


def total(parts):
    acc = parts[0].astype(jnp.float32)
    for part in parts[1:]:
        acc = acc + part.astype(jnp.float32)
    return acc


VMEM = 40 << 20


def gelu(u):
    return 0.5 * u * (1.0 + lax.erf(u * 0.7071067811865476))


def up_kernel(y0, y1, y3, y2_left, y2_right, w, h):
    def put(at, u):
        h[at * 192 : (at + 1) * 192, :] = gelu(u).astype(jnp.bfloat16)

    for at, y in ((0, y0), (1, y1), (3, y3)):
        put(at, jnp.dot(y[...], w[...], preferred_element_type=jnp.float32))
    u = jnp.dot(y2_left[...], w[: D // 2], preferred_element_type=jnp.float32)
    put(2, u + jnp.dot(y2_right[...], w[D // 2 :], preferred_element_type=jnp.float32))


def up_call(rows, w):
    whole = lambda shape: pl.BlockSpec(shape, lambda n: (0, 0))
    return pl.pallas_call(
        up_kernel,
        out_shape=jax.ShapeDtypeStruct((768, 1024), jnp.bfloat16),
        grid=(4,),
        in_specs=[whole(r.shape) for r in rows] + [pl.BlockSpec((D, 256), lambda n: (0, n))],
        out_specs=pl.BlockSpec((768, 256), lambda n: (0, n)),
        compiler_params=pltpu.CompilerParams(vmem_limit_bytes=VMEM),
        cost_estimate=pl.CostEstimate(
            flops=2 * 768 * 1024 * D, bytes_accessed=2 * (768 * D + D * 1024 + 768 * 1024), transcendentals=0
        ),
        name="up",
    )(*rows, w)


def down_kernel(h, d, p0, p1, p2, p3):
    for at, p in ((2, p2), (1, p1), (3, p3), (0, p0)):
        rows = h[at * 192 : (at + 1) * 192, :]
        p[...] = jnp.dot(rows, d[...], preferred_element_type=jnp.float32).astype(jnp.bfloat16)


def down_call(h, d, first, width):
    at = first // width
    return pl.pallas_call(
        down_kernel,
        out_shape=[jax.ShapeDtypeStruct((192, 2 * width), jnp.bfloat16)] * 4,
        grid=(2,),
        in_specs=[
            pl.BlockSpec((768, 1024), lambda n: (0, 0)),
            pl.BlockSpec((1024, width), lambda n: (0, n + at)),
        ],
        out_specs=[pl.BlockSpec((192, width), lambda n: (0, n))] * 4,
        compiler_params=pltpu.CompilerParams(vmem_limit_bytes=VMEM),
        cost_estimate=pl.CostEstimate(
            flops=2 * 768 * 1024 * 2 * width, bytes_accessed=2 * (768 * 1024 + 1792 * 2 * width), transcendentals=0
        ),
        name="down",
    )(h, d)


def split_sum(parts, send):
    half = parts[0].shape[1] // 2
    left = send(parts[2][:, :half], 1)
    right = send(parts[2][:, half:], -1)
    ahead = jnp.concatenate(
        [total([parts[1][:, :half], left]).astype(jnp.bfloat16), parts[1][:, half:]], axis=1
    )
    behind = jnp.concatenate(
        [parts[3][:, :half], total([parts[3][:, half:], right]).astype(jnp.bfloat16)], axis=1
    )
    return total([parts[0], send(ahead, 1), send(behind, -1)])


def local(tokens, routes, router, w_up, w_down, grad_parts, master, moment_one, moment_two):
    here = lax.axis_index("dp")
    x, zl, c = here // 4, (here // 2) % 2, here % 2
    half = D // 2

    up = lax.all_gather(w_up, "dp", axis=0, tiled=True)
    down = lax.all_gather(w_down, "dp", axis=0, tiled=True)

    routed, gating = gating_of(tokens, routes, router)
    slot_index = jnp.cumsum(routed.astype(jnp.int32)) - 1
    slot_iota = jnp.arange(CAP, dtype=jnp.int32)
    picks = ((slot_index[None, :] == slot_iota[:, None]) & routed[None, :]).astype(jnp.bfloat16)
    own = jnp.dot(picks, tokens, preferred_element_type=jnp.float32).astype(jnp.bfloat16)
    near = [get_tensor(own, y=k) for k in (1, 3)]
    far = jnp.concatenate([get_tensor(own, zh=k) for k in (1, 3, 2)], axis=0)
    y0 = jnp.concatenate([own, far], axis=0)
    y1 = jnp.concatenate([near[0], get_tensor(far, y=1)], axis=0)
    y3 = jnp.concatenate([near[1], get_tensor(far, y=3)], axis=0)
    y2_left = get_tensor(y1[:, :half], y=1)
    y2_right = get_tensor(y3[:, half:], y=3)

    grads = grad_parts[0].reshape(8, 2, 64, D)
    keep = lax.dynamic_index_in_dim(grads, c, axis=1, keepdims=False)
    give = lax.dynamic_index_in_dim(grads, 1 - c, axis=1, keepdims=False)
    give, far_seen = lax.optimization_barrier((give, far))
    core_sum = total([keep, get_dp(give, c=1)]).astype(jnp.bfloat16).reshape(512, D)
    hidden = up_call((y0, y1, y3, y2_left, y2_right), up)
    core_sum, hidden = lax.optimization_barrier((core_sum, hidden))
    xgroups = [[dp_of(i, j, k) for i in range(N_X)] for j in range(N_ZL) for k in range(N_C)]
    x_sum = lax.psum_scatter(
        core_sum, "dp", scatter_dimension=0, tiled=True, axis_index_groups=xgroups
    ).reshape(2, 64, D)

    send_y = lambda value, k: get_tensor(value, y=-k)
    owned = []
    for first in (0, half):
        ysum = split_sum(down_call(hidden, down, first, half // 2), send_y)
        ysum = lax.optimization_barrier(ysum.astype(jnp.bfloat16)).reshape(4, CAP, half)
        came = [ysum[0]] + [get_tensor(ysum[i], zh=-k) for i, k in ((1, 1), (2, 3), (3, 2))]
        owned.append(total(came))
    owned = jnp.concatenate(owned, axis=1)
    combined = jnp.take(owned, jnp.clip(slot_index, 0, CAP - 1), axis=0)
    mixed = (combined * gating[:, None]).astype(jnp.bfloat16)

    keep = lax.dynamic_index_in_dim(x_sum, zl, axis=0, keepdims=False)
    give = lax.dynamic_index_in_dim(x_sum, 1 - zl, axis=0, keepdims=False)
    grad_total = total([keep, get_dp(give, zl=1)])
    new_master, new_one, new_two = adam_step(grad_total, master, moment_one, moment_two)
    return (mixed, new_master, new_one, new_two)


def solution(mesh):
    placed = (
        P(("dp", "tensor"), None),
        P(("dp", "tensor"), None),
        P(),
        P("dp", "tensor"),
        P(("tensor", "dp"), None),
        P("dp", "tensor", None),
        P(("tensor", "dp"), None),
        P(("tensor", "dp"), None),
        P(("tensor", "dp"), None),
    )
    return jax.shard_map(
        local,
        mesh=mesh,
        in_specs=placed,
        out_specs=(
            P(("dp", "tensor"), None),
            P(("tensor", "dp"), None),
            P(("tensor", "dp"), None),
            P(("tensor", "dp"), None),
        ),
        check_vma=False,
    )
```

```python
import jax
import jax.numpy as jnp
from jax import lax
from jax.experimental import pallas as pl
from jax.experimental.pallas import tpu as pltpu
from jax.sharding import PartitionSpec as P

CAP = 48
D = 3072
N_X, N_ZL, N_C = 4, 2, 2
N_ZH, N_Y = 4, 4

beta_first = 0.9
beta_second = 0.999
learn_rate = 0.01
decay_rate = 0.1
adam_eps = 1e-08
bias_first = 1.0 - (0.9**10) ** 10
bias_second = 1.0 - (0.999**10) ** 10


def dp_of(x, zl, c):
    return (x % N_X) * 4 + (zl % N_ZL) * 2 + c % N_C


def tensor_of(zh, y):
    return (zh % N_ZH) * 4 + y % N_Y


def get_dp(value, x=0, zl=0, c=0):
    pairs = [
        (dp_of(i + x, j + zl, k + c), dp_of(i, j, k))
        for i in range(N_X)
        for j in range(N_ZL)
        for k in range(N_C)
    ]
    return lax.ppermute(value, "dp", pairs)


def get_tensor(value, zh=0, y=0):
    pairs = [(tensor_of(i + zh, j + y), tensor_of(i, j)) for i in range(N_ZH) for j in range(N_Y)]
    return lax.ppermute(value, "tensor", pairs)


def gating_of(tokens, routes, router):
    logits = jnp.dot(tokens, router, preferred_element_type=jnp.float32)
    expert_iota = jnp.arange(logits.shape[1], dtype=jnp.int32)
    chosen = jnp.sum(jnp.where(routes[:, :, None] == expert_iota, logits[:, None, :], 0.0), axis=2)
    is_first = routes[:, 0] == 0
    routed = is_first | (routes[:, 1] == 0)
    own_logit = jnp.where(is_first, chosen[:, 0], chosen[:, 1])
    partner = jnp.where(is_first, chosen[:, 1], chosen[:, 0])
    gating = jnp.where(routed, jax.nn.sigmoid(own_logit - partner), 0.0)
    return (routed, gating)


def adam_step(grad_total, master, moment_one, moment_two):
    new_one = (
        beta_first * moment_one.astype(jnp.float32) + (1.0 - beta_first) * grad_total
    ).astype(jnp.bfloat16)
    new_two = beta_second * moment_two + (1.0 - beta_second) * grad_total * grad_total
    update = new_one.astype(jnp.float32) / bias_first / (jnp.sqrt(new_two / bias_second) + adam_eps)
    new_master = master - learn_rate * (update + decay_rate * master)
    return (new_master, new_one, new_two)


def total(parts):
    acc = parts[0].astype(jnp.float32)
    for part in parts[1:]:
        acc = acc + part.astype(jnp.float32)
    return acc


VMEM = 40 << 20


def gelu(u):
    return 0.5 * u * (1.0 + lax.erf(u * 0.7071067811865476))


def prep_kernel(routes, tokens, rows):
    routed = jnp.where((routes[0:1, :] == 0) | (routes[1:2, :] == 0), 1.0, 0.0)
    before = lax.broadcasted_iota(jnp.int32, (128, 128), 0) < lax.broadcasted_iota(jnp.int32, (128, 128), 1)
    slot = jnp.dot(routed, jnp.where(before, 1.0, 0.0), preferred_element_type=jnp.float32)
    wanted = lax.broadcasted_iota(jnp.int32, (CAP, 128), 0).astype(jnp.float32)
    picks = jnp.where((wanted == slot) & (routed > 0.5), 1.0, 0.0).astype(jnp.bfloat16)
    for n in range(N_X):
        block = jnp.dot(picks, tokens[:, n * 768 : (n + 1) * 768], preferred_element_type=jnp.float32)
        block = block.astype(jnp.bfloat16)
        cut = [block[:, k * 192 : (k + 1) * 192] for k in (0, 2, 1, 3)]
        rows[:, n * 768 : (n + 1) * 768] = jnp.concatenate(cut, axis=1)


def prep_call(routes, tokens):
    return pl.pallas_call(
        prep_kernel,
        out_shape=jax.ShapeDtypeStruct((CAP, D), jnp.bfloat16),
        in_specs=[pl.BlockSpec(memory_space=pltpu.VMEM)] * 2,
        out_specs=pl.BlockSpec(memory_space=pltpu.VMEM),
        compiler_params=pltpu.CompilerParams(vmem_limit_bytes=16 << 20),
        name="prep",
    )(routes, tokens)


def finish_kernel(routes, gating, *refs):
    parts, out = refs[:8], refs[8]
    routed = jnp.where((routes[:, 0:1] == 0) | (routes[:, 1:2] == 0), 1.0, 0.0)
    before = lax.broadcasted_iota(jnp.int32, (128, 128), 1) < lax.broadcasted_iota(jnp.int32, (128, 128), 0)
    slot = jnp.dot(jnp.where(before, 1.0, 0.0), routed, preferred_element_type=jnp.float32)
    wanted = lax.broadcasted_iota(jnp.int32, (128, CAP), 1).astype(jnp.float32)
    picks = jnp.where((wanted == slot) & (routed > 0.5), 1.0, 0.0).astype(jnp.bfloat16)
    for side in range(2):
        owned = total([p[...] for p in parts[4 * side : 4 * side + 4]])
        high = owned.astype(jnp.bfloat16)
        low = (owned - high.astype(jnp.float32)).astype(jnp.bfloat16)
        taken = jnp.dot(picks, high, preferred_element_type=jnp.float32)
        taken = taken + jnp.dot(picks, low, preferred_element_type=jnp.float32)
        at = side * (D // 2)
        out[:, at : at + D // 2] = (taken * gating[...]).astype(jnp.bfloat16)


def finish_call(routes, gating, parts):
    return pl.pallas_call(
        finish_kernel,
        out_shape=jax.ShapeDtypeStruct((128, D), jnp.bfloat16),
        in_specs=[pl.BlockSpec(memory_space=pltpu.VMEM)] * 10,
        out_specs=pl.BlockSpec(memory_space=pltpu.VMEM),
        compiler_params=pltpu.CompilerParams(vmem_limit_bytes=16 << 20),
        name="finish",
    )(routes, gating, *parts)


def put_hidden(h, at, n, u):
    act = gelu(u).astype(jnp.bfloat16)
    cut = [act[:, k * 64 : (k + 1) * 64] for k in (0, 2, 1, 3)]
    h[at * 192 : (at + 1) * 192, n * 256 : (n + 1) * 256] = jnp.concatenate(cut, axis=1)


def up_kernel(*refs):
    *rows, w, h, held, sems = refs
    copies = [
        pltpu.make_async_copy(w.at[:, n * 256 : (n + 1) * 256], held.at[n], sems.at[n]) for n in range(N_X)
    ]
    for copy in copies:
        copy.start()
    for n in range(N_X):
        copies[n].wait()
        for at, y in enumerate(rows):
            put_hidden(h, at, n, jnp.dot(y[...], held[n], preferred_element_type=jnp.float32))


def up_halves_kernel(left, right, w, h, held, sems):
    copies = [
        pltpu.make_async_copy(w.at[n * 768 : (n + 1) * 768, :], held.at[n], sems.at[n]) for n in range(4)
    ]
    for copy in copies:
        copy.start()
    u = None
    for n in range(4):
        copies[n].wait()
        part = (left, right)[n // 2][:, (n % 2) * 768 : (n % 2 + 1) * 768]
        term = jnp.dot(part, held[n], preferred_element_type=jnp.float32)
        u = term if u is None else u + term
    for n in range(N_X):
        put_hidden(h, 0, n, u[:, n * 256 : (n + 1) * 256])


def up_call(rows, w):
    count = sum(r.shape[0] * r.shape[1] for r in rows) // D
    halves = rows[0].shape[1] < D
    vmem = pl.BlockSpec(memory_space=pltpu.VMEM)
    return pl.pallas_call(
        up_halves_kernel if halves else up_kernel,
        out_shape=jax.ShapeDtypeStruct((count, 1024), jnp.bfloat16),
        in_specs=[vmem] * len(rows) + [pl.BlockSpec(memory_space=pltpu.HBM)],
        out_specs=vmem,
        scratch_shapes=[pltpu.VMEM((4, 768, 1024) if halves else (N_X, D, 256), jnp.bfloat16), pltpu.SemaphoreType.DMA((N_X,))],
        compiler_params=pltpu.CompilerParams(vmem_limit_bytes=12 << 20),
        cost_estimate=pl.CostEstimate(
            flops=2 * count * 1024 * D, bytes_accessed=2 * (count * D + D * 1024 + count * 1024), transcendentals=0
        ),
        name="up",
    )(*rows, w)


def down_kernel(h_near, h_far, d, p0, p1, p2, p3):
    for h, at, p in ((h_far, 0, p2), (h_near, 1, p1), (h_near, 2, p3), (h_near, 0, p0)):
        rows = h[at * 192 : (at + 1) * 192, :]
        p[...] = jnp.dot(rows, d[...], preferred_element_type=jnp.float32).astype(jnp.bfloat16)


def down_call(h_near, h_far, d, first, width):
    at = first // width
    return pl.pallas_call(
        down_kernel,
        out_shape=[jax.ShapeDtypeStruct((192, 2 * width), jnp.bfloat16)] * 4,
        grid=(2,),
        in_specs=[
            pl.BlockSpec((576, 1024), lambda n: (0, 0)),
            pl.BlockSpec((192, 1024), lambda n: (0, 0)),
            pl.BlockSpec((1024, width), lambda n: (0, n + at)),
        ],
        out_specs=[pl.BlockSpec((192, width), lambda n: (0, n))] * 4,
        compiler_params=pltpu.CompilerParams(vmem_limit_bytes=20 << 20),
        cost_estimate=pl.CostEstimate(
            flops=2 * 768 * 1024 * 2 * width, bytes_accessed=2 * (768 * 1024 + 1792 * 2 * width), transcendentals=0
        ),
        name="down",
    )(h_near, h_far, d)


def split_sum(parts, send):
    half = parts[0].shape[1] // 2
    left = send(parts[2][:, :half], 1)
    right = send(parts[2][:, half:], -1)
    ahead = jnp.concatenate(
        [total([parts[1][:, :half], left]).astype(jnp.bfloat16), parts[1][:, half:]], axis=1
    )
    behind = jnp.concatenate(
        [parts[3][:, :half], total([parts[3][:, half:], right]).astype(jnp.bfloat16)], axis=1
    )
    return total([parts[0], send(ahead, 1), send(behind, -1)])


def local(tokens, routes, router, w_up, w_down, grad_parts, master, moment_one, moment_two):
    here = lax.axis_index("dp")
    zl = (here // 2) % 2
    half = D // 2
    tie = lax.optimization_barrier
    groups = [[dp_of(i, j, k) for i in range(N_X) for k in range(N_C)] for j in range(N_ZL)]

    def gathered(value):
        came = get_dp(value, zl=1)
        pair = jnp.concatenate([jnp.where(zl == 0, value, came), jnp.where(zl == 0, came, value)], axis=0)
        return lax.all_gather(pair, "dp", axis=0, tiled=True, axis_index_groups=groups)

    up = gathered(w_up)

    routed, gating = gating_of(tokens, routes, router)
    own = prep_call(routes.T, tokens)
    near = [get_tensor(own, y=k) for k in (1, 3)]
    far = jnp.concatenate([get_tensor(own, zh=k) for k in (1, 3, 2)], axis=0)
    near[0], near[1], w_down = tie((near[0], near[1], w_down))
    far, near[0], near[1] = tie((far, near[0], near[1]))
    down = gathered(w_down)
    y0 = jnp.concatenate([own, far], axis=0)
    y1 = jnp.concatenate([near[0], get_tensor(far, y=1)], axis=0)
    y3 = jnp.concatenate([near[1], get_tensor(far, y=3)], axis=0)
    y0, y1, y3, up = tie((y0, y1, y3, up))
    y2_left = get_tensor(y1[:, :half], y=1)
    y2_right = get_tensor(y3[:, half:], y=3)

    grads, _ = tie((grad_parts[0], far))
    grads = grads.reshape(N_X, N_ZL, N_C, 64, D).transpose(0, 2, 1, 3, 4).reshape(1024, D)

    h_near = up_call((y0, y1, y3), up)
    y2_left, y2_right, h_near = tie((y2_left, y2_right, h_near))
    h_far = up_call((y2_left, y2_right), up)
    grads, h_far = tie((grads, h_far))
    x_sum = lax.psum_scatter(
        grads, "dp", scatter_dimension=0, tiled=True, axis_index_groups=groups
    ).reshape(2, 64, D)

    send_y = lambda value, k: get_tensor(value, y=-k)
    owned = []
    for first in (0, half):
        ysum = split_sum(down_call(h_near, h_far, down, first, half // 2), send_y)
        ysum = lax.optimization_barrier(ysum.astype(jnp.bfloat16)).reshape(4, CAP, half)
        came = [ysum[0]] + [get_tensor(ysum[i], zh=-k) for i, k in ((1, 1), (2, 3), (3, 2))]
        owned += came
    keep = lax.dynamic_index_in_dim(x_sum, zl, axis=0, keepdims=False)
    give = lax.dynamic_index_in_dim(x_sum, 1 - zl, axis=0, keepdims=False)
    grad_total = total([keep, get_dp(give, zl=1)])
    new_master, new_one, new_two = adam_step(grad_total, master, moment_one, moment_two)
    owned[-1], new_master, new_one, new_two = tie((owned[-1], new_master, new_one, new_two))
    mixed = finish_call(routes, gating[:, None], owned)
    return (mixed, new_master, new_one, new_two)


def solution(mesh):
    placed = (
        P(("dp", "tensor"), None),
        P(("dp", "tensor"), None),
        P(),
        P("dp", "tensor"),
        P(("tensor", "dp"), None),
        P("dp", "tensor", None),
        P(("tensor", "dp"), None),
        P(("tensor", "dp"), None),
        P(("tensor", "dp"), None),
    )
    return jax.shard_map(
        local,
        mesh=mesh,
        in_specs=placed,
        out_specs=(
            P(("dp", "tensor"), None),
            P(("tensor", "dp"), None),
            P(("tensor", "dp"), None),
            P(("tensor", "dp"), None),
        ),
        check_vma=False,
    )
```

```python
import jax
import jax.numpy as jnp
from jax import lax
from jax.experimental import pallas as pl
from jax.experimental.pallas import tpu as pltpu
from jax.sharding import PartitionSpec as P

CAP = 48
D = 3072
N_X, N_ZL, N_C = 4, 2, 2
N_ZH, N_Y = 4, 4

beta_first = 0.9
beta_second = 0.999
learn_rate = 0.01
decay_rate = 0.1
adam_eps = 1e-08
bias_first = 1.0 - (0.9**10) ** 10
bias_second = 1.0 - (0.999**10) ** 10


def dp_of(x, zl, c):
    return (x % N_X) * 4 + (zl % N_ZL) * 2 + c % N_C


def tensor_of(zh, y):
    return (zh % N_ZH) * 4 + y % N_Y


def get_dp(value, x=0, zl=0, c=0):
    pairs = [
        (dp_of(i + x, j + zl, k + c), dp_of(i, j, k))
        for i in range(N_X)
        for j in range(N_ZL)
        for k in range(N_C)
    ]
    return lax.ppermute(value, "dp", pairs)


def get_tensor(value, zh=0, y=0):
    pairs = [(tensor_of(i + zh, j + y), tensor_of(i, j)) for i in range(N_ZH) for j in range(N_Y)]
    return lax.ppermute(value, "tensor", pairs)


def gating_of(tokens, routes, router):
    logits = jnp.dot(tokens, router, preferred_element_type=jnp.float32)
    expert_iota = jnp.arange(logits.shape[1], dtype=jnp.int32)
    chosen = jnp.sum(jnp.where(routes[:, :, None] == expert_iota, logits[:, None, :], 0.0), axis=2)
    is_first = routes[:, 0] == 0
    routed = is_first | (routes[:, 1] == 0)
    own_logit = jnp.where(is_first, chosen[:, 0], chosen[:, 1])
    partner = jnp.where(is_first, chosen[:, 1], chosen[:, 0])
    gating = jnp.where(routed, jax.nn.sigmoid(own_logit - partner), 0.0)
    return (routed, gating)


def adam_step(grad_total, master, moment_one, moment_two):
    new_one = (
        beta_first * moment_one.astype(jnp.float32) + (1.0 - beta_first) * grad_total
    ).astype(jnp.bfloat16)
    new_two = beta_second * moment_two + (1.0 - beta_second) * grad_total * grad_total
    update = new_one.astype(jnp.float32) / bias_first / (jnp.sqrt(new_two / bias_second) + adam_eps)
    new_master = master - learn_rate * (update + decay_rate * master)
    return (new_master, new_one, new_two)


def total(parts):
    acc = parts[0].astype(jnp.float32)
    for part in parts[1:]:
        acc = acc + part.astype(jnp.float32)
    return acc


VMEM = 40 << 20


def gelu(u):
    return 0.5 * u * (1.0 + lax.erf(u * 0.7071067811865476))


def prep_kernel(routes, tokens, rows):
    routed = jnp.where((routes[0:1, :] == 0) | (routes[1:2, :] == 0), 1.0, 0.0)
    before = lax.broadcasted_iota(jnp.int32, (128, 128), 0) < lax.broadcasted_iota(jnp.int32, (128, 128), 1)
    slot = jnp.dot(routed, jnp.where(before, 1.0, 0.0), preferred_element_type=jnp.float32)
    wanted = lax.broadcasted_iota(jnp.int32, (CAP, 128), 0).astype(jnp.float32)
    picks = jnp.where((wanted == slot) & (routed > 0.5), 1.0, 0.0).astype(jnp.bfloat16)
    for n in range(N_X):
        block = jnp.dot(picks, tokens[:, n * 768 : (n + 1) * 768], preferred_element_type=jnp.float32)
        block = block.astype(jnp.bfloat16)
        cut = [block[:, k * 192 : (k + 1) * 192] for k in (0, 2, 1, 3)]
        rows[:, n * 768 : (n + 1) * 768] = jnp.concatenate(cut, axis=1)


def prep_call(routes, tokens):
    return pl.pallas_call(
        prep_kernel,
        out_shape=jax.ShapeDtypeStruct((CAP, D), jnp.bfloat16),
        in_specs=[pl.BlockSpec(memory_space=pltpu.VMEM)] * 2,
        out_specs=pl.BlockSpec(memory_space=pltpu.VMEM),
        compiler_params=pltpu.CompilerParams(vmem_limit_bytes=16 << 20),
        name="prep",
    )(routes, tokens)


def finish_kernel(routes, gating, *refs):
    parts, out = refs[:8], refs[8]
    routed = jnp.where((routes[:, 0:1] == 0) | (routes[:, 1:2] == 0), 1.0, 0.0)
    before = lax.broadcasted_iota(jnp.int32, (128, 128), 1) < lax.broadcasted_iota(jnp.int32, (128, 128), 0)
    slot = jnp.dot(jnp.where(before, 1.0, 0.0), routed, preferred_element_type=jnp.float32)
    wanted = lax.broadcasted_iota(jnp.int32, (128, CAP), 1).astype(jnp.float32)
    picks = jnp.where((wanted == slot) & (routed > 0.5), 1.0, 0.0).astype(jnp.bfloat16)
    for side in range(2):
        owned = total([p[...] for p in parts[4 * side : 4 * side + 4]])
        high = owned.astype(jnp.bfloat16)
        low = (owned - high.astype(jnp.float32)).astype(jnp.bfloat16)
        taken = jnp.dot(picks, high, preferred_element_type=jnp.float32)
        taken = taken + jnp.dot(picks, low, preferred_element_type=jnp.float32)
        at = side * (D // 2)
        out[:, at : at + D // 2] = (taken * gating[...]).astype(jnp.bfloat16)


def finish_call(routes, gating, parts):
    return pl.pallas_call(
        finish_kernel,
        out_shape=jax.ShapeDtypeStruct((128, D), jnp.bfloat16),
        in_specs=[pl.BlockSpec(memory_space=pltpu.VMEM)] * 10,
        out_specs=pl.BlockSpec(memory_space=pltpu.VMEM),
        compiler_params=pltpu.CompilerParams(vmem_limit_bytes=16 << 20),
        name="finish",
    )(routes, gating, *parts)


def put_hidden(h, at, n, u):
    act = gelu(u).astype(jnp.bfloat16)
    cut = [act[:, k * 64 : (k + 1) * 64] for k in (0, 2, 1, 3)]
    h[at * 192 : (at + 1) * 192, n * 256 : (n + 1) * 256] = jnp.concatenate(cut, axis=1)


def up_kernel(*refs):
    *rows, w, h, held, sems = refs
    copies = [
        pltpu.make_async_copy(w.at[:, n * 256 : (n + 1) * 256], held.at[n], sems.at[n]) for n in range(N_X)
    ]
    for copy in copies:
        copy.start()
    for n in range(N_X):
        copies[n].wait()
        for at, y in enumerate(rows):
            put_hidden(h, at, n, jnp.dot(y[...], held[n], preferred_element_type=jnp.float32))


def up_halves_kernel(left, right, w, h, held, sems):
    copies = [
        pltpu.make_async_copy(w.at[n * 768 : (n + 1) * 768, :], held.at[n], sems.at[n]) for n in range(4)
    ]
    for copy in copies:
        copy.start()
    u = None
    for n in range(4):
        copies[n].wait()
        part = (left, right)[n // 2][:, (n % 2) * 768 : (n % 2 + 1) * 768]
        term = jnp.dot(part, held[n], preferred_element_type=jnp.float32)
        u = term if u is None else u + term
    for n in range(N_X):
        put_hidden(h, 0, n, u[:, n * 256 : (n + 1) * 256])


def up_call(rows, w):
    count = sum(r.shape[0] * r.shape[1] for r in rows) // D
    halves = rows[0].shape[1] < D
    vmem = pl.BlockSpec(memory_space=pltpu.VMEM)
    return pl.pallas_call(
        up_halves_kernel if halves else up_kernel,
        out_shape=jax.ShapeDtypeStruct((count, 1024), jnp.bfloat16),
        in_specs=[vmem] * len(rows) + [pl.BlockSpec(memory_space=pltpu.HBM)],
        out_specs=vmem,
        scratch_shapes=[pltpu.VMEM((4, 768, 1024) if halves else (N_X, D, 256), jnp.bfloat16), pltpu.SemaphoreType.DMA((N_X,))],
        compiler_params=pltpu.CompilerParams(vmem_limit_bytes=12 << 20),
        cost_estimate=pl.CostEstimate(
            flops=2 * count * 1024 * D, bytes_accessed=2 * (count * D + D * 1024 + count * 1024), transcendentals=0
        ),
        name="up",
    )(*rows, w)


def down_kernel(h_near, h_far, d, p0, p1, p2, p3):
    for h, at, p in ((h_far, 0, p2), (h_near, 1, p1), (h_near, 2, p3), (h_near, 0, p0)):
        rows = h[at * 192 : (at + 1) * 192, :]
        p[...] = jnp.dot(rows, d[...], preferred_element_type=jnp.float32).astype(jnp.bfloat16)


def down_call(h_near, h_far, d, first, width):
    at = first // width
    return pl.pallas_call(
        down_kernel,
        out_shape=[jax.ShapeDtypeStruct((192, 2 * width), jnp.bfloat16)] * 4,
        grid=(2,),
        in_specs=[
            pl.BlockSpec((576, 1024), lambda n: (0, 0)),
            pl.BlockSpec((192, 1024), lambda n: (0, 0)),
            pl.BlockSpec((1024, width), lambda n: (0, n + at)),
        ],
        out_specs=[pl.BlockSpec((192, width), lambda n: (0, n))] * 4,
        compiler_params=pltpu.CompilerParams(vmem_limit_bytes=20 << 20),
        cost_estimate=pl.CostEstimate(
            flops=2 * 768 * 1024 * 2 * width, bytes_accessed=2 * (768 * 1024 + 1792 * 2 * width), transcendentals=0
        ),
        name="down",
    )(h_near, h_far, d)


def split_sum(parts, send):
    half = parts[0].shape[1] // 2
    left = send(parts[2][:, :half], 1)
    right = send(parts[2][:, half:], -1)
    ahead = jnp.concatenate(
        [total([parts[1][:, :half], left]).astype(jnp.bfloat16), parts[1][:, half:]], axis=1
    )
    behind = jnp.concatenate(
        [parts[3][:, :half], total([parts[3][:, half:], right]).astype(jnp.bfloat16)], axis=1
    )
    return total([parts[0], send(ahead, 1), send(behind, -1)])


def local(tokens, routes, router, w_up, w_down, grad_parts, master, moment_one, moment_two):
    here = lax.axis_index("dp")
    zl = (here // 2) % 2
    half = D // 2
    tie = lax.optimization_barrier
    groups = [[dp_of(i, j, k) for i in range(N_X) for k in range(N_C)] for j in range(N_ZL)]

    def gathered(value):
        came = get_dp(value, zl=1)
        pair = jnp.concatenate([value, value], axis=0)
        pair = lax.dynamic_update_slice_in_dim(pair, came, (1 - zl) * value.shape[0], axis=0)
        return lax.all_gather(pair, "dp", axis=0, tiled=True, axis_index_groups=groups)

    up = gathered(w_up)

    routed, gating = gating_of(tokens, routes, router)
    own = prep_call(routes.T, tokens)
    near = [get_tensor(own, y=k) for k in (1, 3)]
    far = jnp.concatenate([get_tensor(own, zh=k) for k in (1, 3, 2)], axis=0)
    near[0], near[1], w_down = tie((near[0], near[1], w_down))
    far, near[0], near[1] = tie((far, near[0], near[1]))
    down = gathered(w_down)
    y0 = jnp.concatenate([own, far], axis=0)
    y1 = jnp.concatenate([near[0], get_tensor(far, y=1)], axis=0)
    y3 = jnp.concatenate([near[1], get_tensor(far, y=3)], axis=0)
    y0, y1, y3, up = tie((y0, y1, y3, up))
    y2_left = get_tensor(y1[:, :half], y=1)
    y2_right = get_tensor(y3[:, half:], y=3)

    grads, _ = tie((grad_parts[0], far))
    grads = grads.reshape(N_X, N_ZL, N_C, 64, D).transpose(0, 2, 1, 3, 4).reshape(1024, D)

    h_near = up_call((y0, y1, y3), up)
    y2_left, y2_right, h_near = tie((y2_left, y2_right, h_near))
    h_far = up_call((y2_left, y2_right), up)
    grads, h_far = tie((grads, h_far))
    x_sum = lax.psum_scatter(
        grads, "dp", scatter_dimension=0, tiled=True, axis_index_groups=groups
    ).reshape(2, 64, D)

    send_y = lambda value, k: get_tensor(value, y=-k)
    owned = []
    for first in (0, half):
        ysum = split_sum(down_call(h_near, h_far, down, first, half // 2), send_y)
        ysum = lax.optimization_barrier(ysum.astype(jnp.bfloat16)).reshape(4, CAP, half)
        came = [ysum[0]] + [get_tensor(ysum[i], zh=-k) for i, k in ((1, 1), (2, 3), (3, 2))]
        owned += came
    keep = lax.dynamic_index_in_dim(x_sum, zl, axis=0, keepdims=False)
    give = lax.dynamic_index_in_dim(x_sum, 1 - zl, axis=0, keepdims=False)
    grad_total = total([keep, get_dp(give, zl=1)])
    new_master, new_one, new_two = adam_step(grad_total, master, moment_one, moment_two)
    mixed = finish_call(routes, gating[:, None], owned)
    return (mixed, new_master, new_one, new_two)


def solution(mesh):
    placed = (
        P(("dp", "tensor"), None),
        P(("dp", "tensor"), None),
        P(),
        P("dp", "tensor"),
        P(("tensor", "dp"), None),
        P("dp", "tensor", None),
        P(("tensor", "dp"), None),
        P(("tensor", "dp"), None),
        P(("tensor", "dp"), None),
    )
    return jax.shard_map(
        local,
        mesh=mesh,
        in_specs=placed,
        out_specs=(
            P(("dp", "tensor"), None),
            P(("tensor", "dp"), None),
            P(("tensor", "dp"), None),
            P(("tensor", "dp"), None),
        ),
        check_vma=False,
    )
```
